32 devices in a mesh: row: 4 (over y, x), col: 8 (over z, core).
Axes of the slice: x: 2, y: 2, z: 4, core: 2. Of those that a mesh axis runs over, the one named last changes fastest.
Arguments:
- images: float32 [64, 3, 1024], P(('row', 'col')), may hold values from -16 to 16
- roots: int32 [2, 8], replicated, may hold values from 0 to 3, as said below
Outputs:
- kernel_tiles: float32 [2, 8, 16], P(None, 'row', 'col')
The draws below stay inside these ranges and needn't reach their ends.
Inputs may be any that keep to these rules, and one draw needn't show every extreme that they name: `roots`: at each tile index every row group appears for exactly 8 / 4 column groups.
All inputs are finite; a program needn't handle non-finite values.
Results may differ from the reference program's by a relative error of at most 0.0001.
Values sent between devices are 32-bit elements; how exact they have to be, the bound alone decides.
No kernel may reach another device: no remote copies, remote signals or barrier semaphores. Data moves between devices by JAX's collectives and lax.ppermute only.
A program may use at most 64 MiB of HBM per device.

```python
import math
import jax
import jax.numpy as jnp
from jax import lax

HEIGHT = 32
WIDTH = 32
CH = 3
DEPTH = 4
STEPS = 2
BLOCK = 2
PIX = 1024
IMAGES = 64
N_ROW = 4
N_COL = 8


def draw_images(key, part):
    keys = jax.random.split(jax.random.fold_in(key, 3), 16)
    pixel_index = jnp.arange(PIX).astype(jnp.int32)
    row_int = (pixel_index // WIDTH).reshape(1, 1, PIX)
    col_int = (pixel_index % WIDTH).reshape(1, 1, PIX)
    row_pos = row_int.astype(jnp.float32)
    col_pos = col_int.astype(jnp.float32)
    log_scale = jax.random.uniform(keys[0], (IMAGES, 1, 1), jnp.float32, math.log(0.5), math.log(1.8))
    means = 0.5 * jax.random.truncated_normal(keys[1], -3.0, 3.0, (IMAGES, CH, 1), jnp.float32)
    noise = 0.3 * jax.random.truncated_normal(keys[2], -3.0, 3.0, (IMAGES, CH, PIX), jnp.float32)
    freq_lo = math.log(0.15)
    freq_hi = math.log(1.0)
    amp_lo = math.log(0.4)
    waves = jnp.zeros((IMAGES, CH, PIX), jnp.float32)
    for wave_index in range(3):
        base = 3 + 3 * wave_index
        wave_keys = jax.random.split(keys[base], 5)
        freq = jnp.exp(jax.random.uniform(wave_keys[0], (IMAGES, 1, 1), jnp.float32, freq_lo, freq_hi))
        turn = jax.random.uniform(wave_keys[1], (IMAGES, 1, 1), jnp.float32, 0.0, math.pi)
        phase = jax.random.uniform(wave_keys[2], (IMAGES, 1, 1), jnp.float32, -math.pi, math.pi)
        amplitude = jnp.exp(jax.random.uniform(wave_keys[3], (IMAGES, 1, 1), jnp.float32, amp_lo, math.log(1.5)))
        mixing = jax.random.uniform(wave_keys[4], (IMAGES, CH, 1), jnp.float32, 0.4, 1.0)
        argument = freq * (jnp.cos(turn) * row_pos + jnp.sin(turn) * col_pos) + phase
        waves = waves + amplitude * mixing * jnp.cos(argument)
    top = jax.random.randint(keys[12], (IMAGES, 1, 1), 0, HEIGHT - 4)
    left = jax.random.randint(keys[13], (IMAGES, 1, 1), 0, WIDTH - 4)
    extent = jax.random.randint(keys[14], (IMAGES, 2, 1), 6, 17)
    inside = (row_int >= top) & (row_int < top + extent[:, 0:1]) & (col_int >= left) & (col_int < left + extent[:, 1:2])
    patch_amp = jax.random.uniform(keys[15], (IMAGES, CH, 1), jnp.float32, -1.5, 1.5)
    patch = jnp.where(inside, patch_amp, 0.0)
    return (jnp.exp(log_scale) * (means + waves + patch + noise)).astype(jnp.float32)


def draw_roots(key, part):
    keys = jax.random.split(jax.random.fold_in(key, 7), STEPS)
    orders = jax.vmap(lambda subkey: jax.random.permutation(subkey, N_COL))(keys)
    return (orders % N_ROW).astype(jnp.int32)


def setup_inputs(seed: int = 0) -> dict:
    key_list = jax.random.split(jax.random.key(seed), 3)
    return {
        "images": draw_images(jax.random.fold_in(key_list[2], 71), 0),
        "roots": draw_roots(jax.random.fold_in(key_list[2], 71), 0),
    }


weight_var = 2.0
bias_var = 0.1

def box_sum(maps):
    leading = maps.shape[:-1]
    grid = maps.reshape(leading + (HEIGHT, WIDTH))
    padded = jnp.pad(grid, [(0, 0)] * len(leading) + [(1, 1), (1, 1)])
    total = jnp.zeros_like(grid)
    for offset_h in range(3):
        for offset_w in range(3):
            total = total + padded[..., offset_h:offset_h + HEIGHT, offset_w:offset_w + WIDTH]
    return total.reshape(maps.shape)

def relu_map(cross, self_a, self_b):
    scale_ab = jnp.sqrt(self_a * self_b)
    cosine = cross / scale_ab
    return scale_ab * (jnp.sqrt(1.0 - cosine * cosine) + (math.pi - jnp.arccos(cosine)) * cosine) / (2.0 * math.pi)

def self_maps(pictures):
    energy = lax.optimization_barrier(jnp.sum(pictures * pictures, axis=1))
    level = weight_var / (9.0 * CH) * box_sum(energy) + bias_var
    stacked = [level]
    for depth_level in range(DEPTH - 1):
        level = weight_var / 9.0 * box_sum(0.5 * level) + bias_var
        stacked.append(level)
    return jnp.stack(stacked, axis=1)

def pair_kernel(row_pictures, col_pictures, row_selfs, col_selfs):
    cross = jnp.einsum('acp,bcp->abp', row_pictures, col_pictures, precision=lax.Precision.HIGHEST)
    level = weight_var / (9.0 * CH) * box_sum(cross) + bias_var
    for depth_level in range(DEPTH - 1):
        mapped = relu_map(level, row_selfs[:, None, depth_level], col_selfs[None, :, depth_level])
        level = weight_var / 9.0 * box_sum(mapped) + bias_var
    final = relu_map(level, row_selfs[:, None, DEPTH - 1], col_selfs[None, :, DEPTH - 1])
    return weight_var * lax.optimization_barrier(jnp.mean(final, axis=-1)) + bias_var

def reference(images, roots):
    blocks = images.reshape(N_ROW, N_COL, BLOCK, CH, PIX)
    selfs = self_maps(images).reshape(N_ROW, N_COL, BLOCK, DEPTH, PIX)
    columns = jnp.arange(N_COL).astype(jnp.int32)
    outputs = []
    for turn_index in range(STEPS):
        row_blocks = blocks[roots[turn_index], columns]
        row_selfs = selfs[roots[turn_index], columns]

        def one_group(packed):
            block_row, self_row = packed
            col_blocks = jnp.roll(block_row, turn_index + 1, axis=0)
            col_selfs = jnp.roll(self_row, turn_index + 1, axis=0)
            return jax.vmap(pair_kernel)(row_blocks, col_blocks, row_selfs, col_selfs)
        tiles = lax.map(one_group, (blocks, selfs))
        outputs.append(tiles.transpose(0, 2, 1, 3).reshape(N_ROW * BLOCK, N_COL * BLOCK))
    return jnp.stack(outputs)
```

```python
import math

import jax
import jax.numpy as jnp
import numpy as np
from jax import lax
from jax.experimental import pallas as pl
from jax.experimental.pallas import tpu as pltpu
from jax.sharding import PartitionSpec as P

WIDTH = 32
LANES = 128
DEPTH = 4

weight_var = 2.0
bias_var = 0.1


def remainder_coefficients(degree=6, nodes=64):
    u = 0.5 + 0.5 * np.cos(np.pi * (np.arange(nodes) + 0.5) / nodes)
    angle = 2.0 * np.arcsin(np.sqrt(0.5 * u))
    series = sum(
        (-1) ** n * 2.0 * n / math.factorial(2 * n + 1) * angle ** (2 * n + 1) * -1.0
        for n in range(1, 8)
    )
    exact = np.sin(angle) - angle * np.cos(angle)
    q = np.where(angle < 0.5, series, exact) / u**1.5
    fit = np.polynomial.chebyshev.Chebyshev.fit(u, q, degree, domain=[0.0, 1.0])
    return fit.convert(kind=np.polynomial.Polynomial).coef


COEFS = [float(v) / (2.0 * math.pi) for v in remainder_coefficients()]


def kernel(powers, n_row, roots_ref, *refs):
    n_tiles = roots_ref.shape[0]
    row_refs, col_refs, out_ref = refs[:n_row], refs[n_row:-1], refs[-1]
    row_index, col_index = lax.axis_index("row"), lax.axis_index("col")
    block = row_refs[0].shape[0] // 24
    rows = 8 * block
    sub = lax.broadcasted_iota(jnp.int32, (rows, LANES), 0)
    lane = lax.broadcasted_iota(jnp.int32, (rows, LANES), 1)
    not_left = (lane % WIDTH) != 0
    not_right = (lane % WIDTH) != WIDTH - 1
    first_band = lane < WIDTH
    last_band = lane >= LANES - WIDTH
    above_inside = jnp.logical_and(first_band, sub >= block)
    below_inside = jnp.logical_and(last_band, sub < rows - block)
    even = (sub % 2) == 0

    def box(m):
        left = jnp.where(not_left, pltpu.roll(m, 1, 1), 0.0)
        right = jnp.where(not_right, pltpu.roll(m, LANES - 1, 1), 0.0)
        across = m + left + right
        down = pltpu.roll(across, WIDTH, 1)
        up = pltpu.roll(across, LANES - WIDTH, 1)
        down_far = jnp.where(above_inside, pltpu.roll(down, block, 0), 0.0)
        up_far = jnp.where(below_inside, pltpu.roll(up, rows - block, 0), 0.0)
        return across + jnp.where(first_band, down_far, down) + jnp.where(last_band, up_far, up)

    def swapped(m):
        return jnp.where(even, pltpu.roll(m, rows - 1, 0), pltpu.roll(m, 1, 0))

    def channels(value):
        return [value[c * rows:(c + 1) * rows] for c in range(3)]

    def self_maps(value):
        energy = sum(v * v for v in channels(value))
        level = weight_var / 27.0 * box(energy) + bias_var
        levels = [level]
        for _ in range(DEPTH - 1):
            level = box(weight_var / 18.0 * level) + bias_var
            levels.append(level)
        inverse = [lax.rsqrt(v) for v in levels]
        return [v * r for v, r in zip(levels, inverse)], inverse

    def relu_map(k, scale, inverse):
        c = k * inverse
        u = jnp.maximum(1.0 - jnp.abs(c), 0.0)
        poly = jnp.full_like(u, COEFS[-1])
        for coef in COEFS[-2::-1]:
            poly = poly * u + coef
        return 0.5 * jnp.maximum(k, 0.0) + scale * (u * jnp.sqrt(u)) * poly

    sums = []
    for s in range(n_tiles):
        root = roots_ref[s, col_index]
        source = root ^ row_index if powers else lax.rem(row_index - root + n_row, n_row)
        row_value = row_refs[0][...]
        for k in range(1, n_row):
            row_value = jnp.where(source == k, row_refs[k][...], row_value)
        col_value = col_refs[s][...]
        row_std, row_inv = self_maps(row_value)
        col_std, col_inv = self_maps(col_value)
        for d in range(2):
            if d:
                col_std = [swapped(v) for v in col_std]
                col_inv = [swapped(v) for v in col_inv]
            turn = swapped if d else lambda v: v
            cross = sum(a * turn(b) for a, b in zip(channels(row_value), channels(col_value)))
            level = weight_var / 27.0 * box(cross) + bias_var
            for l in range(DEPTH):
                mapped = relu_map(level, row_std[l] * col_std[l], row_inv[l] * col_inv[l])
                if l < DEPTH - 1:
                    level = weight_var / 9.0 * box(mapped) + bias_var
            total = mapped[:8] + mapped[8:]
            total = total + pltpu.roll(total, 4, 0)
            sums.append(total + pltpu.roll(total, 2, 0))
    sub8 = sub[:8]
    packed = sums[0]
    for q in range(8):
        s, a, b = (q // 2) % 2, q % 2, q // 4
        packed = jnp.where(sub8 == q, sums[2 * s + (a ^ b)], packed)
    mean = jnp.sum(packed, axis=1, keepdims=True) * (1.0 / 1024.0)
    value = jnp.broadcast_to(weight_var * mean + bias_var, (8, LANES))
    result = jnp.where(lane[:8] == 0, value, pltpu.roll(value, 4, 0))
    for s in range(n_tiles):
        out_ref[s] = result[2 * s:2 * s + 2, 0:2]


def local(images, roots):
    n_row, n_col = lax.axis_size("row"), lax.axis_size("col")
    n_tiles = roots.shape[0]
    block, ch, pix = images.shape
    tiles = pix // LANES
    packed = images.reshape(block, ch, tiles, LANES).transpose(1, 2, 0, 3).reshape(ch * tiles * block, LANES)
    powers = n_row & (n_row - 1) == 0
    row_blocks = [packed]
    for k in range(1, n_row):
        if powers:
            route = [(i, i ^ k) for i in range(n_row)]
        else:
            route = [(i, (i + k) % n_row) for i in range(n_row)]
        row_blocks.append(lax.ppermute(packed, "row", route))
    col_blocks = [
        lax.ppermute(packed, "col", [(i, (i + s + 1) % n_col) for i in range(n_col)])
        for s in range(n_tiles)
    ]
    vmem = pl.BlockSpec(memory_space=pltpu.VMEM)
    return pl.pallas_call(
        lambda *refs: kernel(powers, n_row, *refs),
        out_shape=jax.ShapeDtypeStruct((n_tiles, block, block), jnp.float32),
        in_specs=[pl.BlockSpec(memory_space=pltpu.SMEM)] + [vmem] * (n_row + n_tiles),
        out_specs=vmem,
        name="tiles",
    )(roots, *row_blocks, *col_blocks)


def solution(mesh):
    in_specs = (P(("row", "col"), None, None), P())
    out_specs = P(None, "row", "col")
    return jax.shard_map(local, mesh=mesh, in_specs=in_specs, out_specs=out_specs, check_vma=False)
```

```python
import math

import jax
import jax.numpy as jnp
import numpy as np
from jax import lax
from jax.experimental import pallas as pl
from jax.experimental.pallas import tpu as pltpu
from jax.sharding import PartitionSpec as P

WIDTH = 32
LANES = 128
DEPTH = 4

weight_var = 2.0
bias_var = 0.1


def remainder_coefficients(degree=6, nodes=64):
    u = 0.5 + 0.5 * np.cos(np.pi * (np.arange(nodes) + 0.5) / nodes)
    angle = 2.0 * np.arcsin(np.sqrt(0.5 * u))
    series = sum(
        (-1) ** n * 2.0 * n / math.factorial(2 * n + 1) * angle ** (2 * n + 1) * -1.0
        for n in range(1, 8)
    )
    exact = np.sin(angle) - angle * np.cos(angle)
    q = np.where(angle < 0.5, series, exact) / u**1.5
    fit = np.polynomial.chebyshev.Chebyshev.fit(u, q, degree, domain=[0.0, 1.0])
    return fit.convert(kind=np.polynomial.Polynomial).coef


COEFS = [float(v) / (2.0 * math.pi) for v in remainder_coefficients()]


def kernel(powers, n_row, roots_ref, *refs):
    n_tiles = roots_ref.shape[0]
    row_refs, col_refs, out_ref = refs[:n_row], refs[n_row:-1], refs[-1]
    row_index, col_index = lax.axis_index("row"), lax.axis_index("col")
    block = row_refs[0].shape[0] // 24
    rows = 8 * block
    sub = lax.broadcasted_iota(jnp.int32, (rows, LANES), 0)
    lane = lax.broadcasted_iota(jnp.int32, (rows, LANES), 1)
    not_left = (lane % WIDTH) != 0
    not_right = (lane % WIDTH) != WIDTH - 1
    first_band = lane < WIDTH
    last_band = lane >= LANES - WIDTH
    above_inside = jnp.logical_and(first_band, sub >= block)
    below_inside = jnp.logical_and(last_band, sub < rows - block)
    even = (sub % 2) == 0

    def box(m):
        left = jnp.where(not_left, pltpu.roll(m, 1, 1), 0.0)
        right = jnp.where(not_right, pltpu.roll(m, LANES - 1, 1), 0.0)
        across = m + left + right
        down = pltpu.roll(across, WIDTH, 1)
        up = pltpu.roll(across, LANES - WIDTH, 1)
        down_far = jnp.where(above_inside, pltpu.roll(down, block, 0), 0.0)
        up_far = jnp.where(below_inside, pltpu.roll(up, rows - block, 0), 0.0)
        return across + jnp.where(first_band, down_far, down) + jnp.where(last_band, up_far, up)

    def swapped(m):
        return jnp.where(even, pltpu.roll(m, rows - 1, 0), pltpu.roll(m, 1, 0))

    def channels(value):
        return [value[c * rows:(c + 1) * rows] for c in range(3)]

    def self_maps(value):
        energy = sum(v * v for v in channels(value))
        level = weight_var / 27.0 * box(energy) + bias_var
        levels = [level]
        for _ in range(DEPTH - 1):
            level = box(weight_var / 18.0 * level) + bias_var
            levels.append(level)
        inverse = [lax.rsqrt(v) for v in levels]
        return [v * r for v, r in zip(levels, inverse)], inverse

    def relu_map(k, scale, inverse):
        c = k * inverse
        u = jnp.maximum(1.0 - jnp.abs(c), 0.0)
        poly = jnp.full_like(u, COEFS[-1])
        for coef in COEFS[-2::-1]:
            poly = poly * u + coef
        return 0.5 * jnp.maximum(k, 0.0) + scale * (u * jnp.sqrt(u)) * poly

    sums = []
    for s in range(n_tiles):
        root = roots_ref[s, col_index]
        source = root ^ row_index if powers else lax.rem(row_index - root + n_row, n_row)
        row_value = row_refs[0][...]
        for k in range(1, n_row):
            row_value = jnp.where(source == k, row_refs[k][...], row_value)
        col_value = col_refs[s][...]
        row_std, row_inv = self_maps(row_value)
        col_std, col_inv = self_maps(col_value)
        for d in range(2):
            if d:
                col_std = [swapped(v) for v in col_std]
                col_inv = [swapped(v) for v in col_inv]
            turn = swapped if d else lambda v: v
            cross = sum(a * turn(b) for a, b in zip(channels(row_value), channels(col_value)))
            level = weight_var / 27.0 * box(cross) + bias_var
            for l in range(DEPTH):
                mapped = relu_map(level, row_std[l] * col_std[l], row_inv[l] * col_inv[l])
                if l < DEPTH - 1:
                    level = weight_var / 9.0 * box(mapped) + bias_var
            total = mapped[:8] + mapped[8:]
            total = total + pltpu.roll(total, 4, 0)
            sums.append(total + pltpu.roll(total, 2, 0))
    sub8 = sub[:8]
    packed = sums[0]
    for q in range(8):
        s, a, b = (q // 2) % 2, q % 2, q // 4
        packed = jnp.where(sub8 == q, sums[2 * s + (a ^ b)], packed)
    mean = jnp.sum(packed, axis=1, keepdims=True) * (1.0 / 1024.0)
    value = jnp.broadcast_to(weight_var * mean + bias_var, (8, LANES))
    result = jnp.where(lane[:8] == 0, value, pltpu.roll(value, 4, 0))
    for s in range(n_tiles):
        out_ref[s] = result[2 * s:2 * s + 2, 0:2]


def local(images, roots):
    n_row, n_col = lax.axis_size("row"), lax.axis_size("col")
    n_tiles = roots.shape[0]
    block, ch, pix = images.shape
    tiles = pix // LANES
    packed = images.reshape(block, ch, tiles, LANES).transpose(1, 2, 0, 3).reshape(ch * tiles * block, LANES)
    powers = n_row & (n_row - 1) == 0
    row_blocks = [packed]
    for k in range(1, n_row):
        if powers:
            route = [(i, i ^ k) for i in range(n_row)]
        else:
            route = [(i, (i + k) % n_row) for i in range(n_row)]
        row_blocks.append(lax.ppermute(packed, "row", route))
    col_blocks = [
        lax.ppermute(packed, "col", [(i, (i + s + 1) % n_col) for i in range(n_col)])
        for s in range(n_tiles)
    ]
    vmem = pl.BlockSpec(memory_space=pltpu.VMEM)
    return pl.pallas_call(
        lambda *refs: kernel(powers, n_row, *refs),
        out_shape=jax.ShapeDtypeStruct((n_tiles, block, block), jnp.float32),
        in_specs=[pl.BlockSpec(memory_space=pltpu.SMEM)] + [vmem] * (n_row + n_tiles),
        out_specs=vmem,
        name="tiles",
    )(roots, packed, *[pltpu.with_memory_space_constraint(b, pltpu.VMEM) for b in row_blocks[1:] + col_blocks])


def solution(mesh):
    in_specs = (P(("row", "col"), None, None), P())
    out_specs = P(None, "row", "col")
    return jax.shard_map(local, mesh=mesh, in_specs=in_specs, out_specs=out_specs, check_vma=False)
```

```python
import math

import jax
import jax.numpy as jnp
import numpy as np
from jax import lax
from jax.experimental import pallas as pl
from jax.experimental.pallas import tpu as pltpu
from jax.sharding import PartitionSpec as P

WIDTH = 32
LANES = 128
DEPTH = 4

weight_var = 2.0
bias_var = 0.1


def remainder_coefficients(degree=6, nodes=64):
    u = 0.5 + 0.5 * np.cos(np.pi * (np.arange(nodes) + 0.5) / nodes)
    angle = 2.0 * np.arcsin(np.sqrt(0.5 * u))
    series = sum(
        (-1) ** n * 2.0 * n / math.factorial(2 * n + 1) * angle ** (2 * n + 1) * -1.0
        for n in range(1, 8)
    )
    exact = np.sin(angle) - angle * np.cos(angle)
    q = np.where(angle < 0.5, series, exact) / u**1.5
    fit = np.polynomial.chebyshev.Chebyshev.fit(u, q, degree, domain=[0.0, 1.0])
    return fit.convert(kind=np.polynomial.Polynomial).coef


COEFS = [float(v) / (2.0 * math.pi) for v in remainder_coefficients()]


class Stencil:
    def __init__(self, rows, block):
        self.rows, self.block = rows, block
        sub = lax.broadcasted_iota(jnp.int32, (rows, LANES), 0)
        lane = lax.broadcasted_iota(jnp.int32, (rows, LANES), 1)
        self.not_left = (lane % WIDTH) != 0
        self.not_right = (lane % WIDTH) != WIDTH - 1
        self.first_band = lane < WIDTH
        self.last_band = lane >= LANES - WIDTH
        self.above_inside = jnp.logical_and(self.first_band, sub >= block)
        self.below_inside = jnp.logical_and(self.last_band, sub < rows - block)
        self.even = (sub % 2) == 0
        self.sub, self.lane = sub, lane

    def box(self, m):
        left = jnp.where(self.not_left, pltpu.roll(m, 1, 1), 0.0)
        right = jnp.where(self.not_right, pltpu.roll(m, LANES - 1, 1), 0.0)
        across = m + left + right
        down = pltpu.roll(across, WIDTH, 1)
        up = pltpu.roll(across, LANES - WIDTH, 1)
        down_far = jnp.where(self.above_inside, pltpu.roll(down, self.block, 0), 0.0)
        up_far = jnp.where(self.below_inside, pltpu.roll(up, self.rows - self.block, 0), 0.0)
        return across + jnp.where(self.first_band, down_far, down) + jnp.where(self.last_band, up_far, up)

    def swapped(self, m):
        return jnp.where(self.even, pltpu.roll(m, self.rows - 1, 0), pltpu.roll(m, 1, 0))

    def channels(self, value):
        return [value[c * self.rows:(c + 1) * self.rows] for c in range(3)]

    def self_maps(self, value):
        energy = sum(v * v for v in self.channels(value))
        level = weight_var / 27.0 * self.box(energy) + bias_var
        levels = [level]
        for _ in range(DEPTH - 1):
            level = self.box(weight_var / 18.0 * level) + bias_var
            levels.append(level)
        inverse = [lax.rsqrt(v) for v in levels]
        return [v * r for v, r in zip(levels, inverse)], inverse


def prepare(powers, n_row, roots_ref, own_ref, *refs):
    n_tiles = roots_ref.shape[0]
    col_refs, (own_out, source_out, images_out, std_out, inv_out) = refs[:n_tiles], refs[n_tiles:]
    row_index, col_index = lax.axis_index("row"), lax.axis_index("col")
    block = own_ref.shape[0] // 24
    st = Stencil(8 * block, block)
    own_out[...] = own_ref[...]
    for s in range(n_tiles):
        root = roots_ref[s, col_index]
        source = root ^ row_index if powers else lax.rem(row_index - root + n_row, n_row)
        source_out[s] = jnp.full((8, LANES), source, jnp.int32)
        value = col_refs[s][...]
        std, inv = st.self_maps(value)
        for d in range(2):
            turn = st.swapped if d else lambda v: v
            for c, v in enumerate(st.channels(value)):
                images_out[s, d, c] = turn(v)
            for l in range(DEPTH):
                std_out[s, d, l] = turn(std[l])
                inv_out[s, d, l] = turn(inv[l])


def kernel(n_tiles, order, source_ref, images_ref, std_ref, inv_ref, *refs):
    row_refs, out_ref = refs[:-1], refs[-1]
    block = row_refs[0].shape[0] // 24
    st = Stencil(8 * block, block)

    def relu_map(k, scale, inverse):
        c = k * inverse
        u = jnp.maximum(1.0 - jnp.abs(c), 0.0)
        poly = jnp.full_like(u, COEFS[-1])
        for coef in COEFS[-2::-1]:
            poly = poly * u + coef
        return 0.5 * jnp.maximum(k, 0.0) + scale * (u * jnp.sqrt(u)) * poly

    sums = []
    for s in range(n_tiles):
        source = source_ref[s]
        row_value = row_refs[0][...].reshape(-1, 8, LANES)
        for n, k in enumerate(order, 1):
            row_value = jnp.where((source == k)[None], row_refs[n][...].reshape(-1, 8, LANES), row_value)
        row_value = row_value.reshape(-1, LANES)
        row_std, row_inv = st.self_maps(row_value)
        for d in range(2):
            cross = sum(a * images_ref[s, d, c] for c, a in enumerate(st.channels(row_value)))
            level = weight_var / 27.0 * st.box(cross) + bias_var
            for l in range(DEPTH):
                mapped = relu_map(level, row_std[l] * std_ref[s, d, l], row_inv[l] * inv_ref[s, d, l])
                if l < DEPTH - 1:
                    level = weight_var / 9.0 * st.box(mapped) + bias_var
            total = mapped[:8] + mapped[8:]
            total = total + pltpu.roll(total, 4, 0)
            sums.append(total + pltpu.roll(total, 2, 0))
    sub8 = st.sub[:8]
    packed = sums[0]
    for q in range(8):
        s, a, b = (q // 2) % 2, q % 2, q // 4
        packed = jnp.where(sub8 == q, sums[2 * s + (a ^ b)], packed)
    mean = jnp.sum(packed, axis=1, keepdims=True) * (1.0 / 1024.0)
    value = jnp.broadcast_to(weight_var * mean + bias_var, (8, LANES))
    result = jnp.where(st.lane[:8] == 0, value, pltpu.roll(value, 4, 0))
    for s in range(n_tiles):
        out_ref[s] = result[2 * s:2 * s + 2, 0:2]


def local(images, roots):
    n_row, n_col = lax.axis_size("row"), lax.axis_size("col")
    n_tiles = roots.shape[0]
    block, ch, pix = images.shape
    tiles = pix // LANES
    packed = images.reshape(block, ch, tiles, LANES).transpose(1, 2, 0, 3).reshape(ch * tiles * block, LANES)
    powers = n_row & (n_row - 1) == 0
    row_blocks = [packed]
    order = list(range(n_row - 1, 0, -1))
    for k in order:
        if powers:
            route = [(i, i ^ k) for i in range(n_row)]
        else:
            route = [(i, (i + k) % n_row) for i in range(n_row)]
        row_blocks.append(lax.ppermute(packed, "row", route))
    col_blocks = [
        lax.ppermute(packed, "col", [(i, (i + s + 1) % n_col) for i in range(n_col)])
        for s in range(n_tiles)
    ]
    vmem = pl.BlockSpec(memory_space=pltpu.VMEM)
    rows = 8 * block

    def placed(value):
        return pltpu.with_memory_space_constraint(value, pltpu.VMEM)

    own, *made = pl.pallas_call(
        lambda *refs: prepare(powers, n_row, *refs),
        out_shape=[
            pltpu.VMEM(packed.shape, jnp.float32),
            pltpu.VMEM((n_tiles, 8, LANES), jnp.int32),
            pltpu.VMEM((n_tiles, 2, ch, rows, LANES), jnp.float32),
            pltpu.VMEM((n_tiles, 2, DEPTH, rows, LANES), jnp.float32),
            pltpu.VMEM((n_tiles, 2, DEPTH, rows, LANES), jnp.float32),
        ],
        in_specs=[pl.BlockSpec(memory_space=pltpu.SMEM)] + [vmem] * (1 + n_tiles),
        out_specs=[vmem] * 5,
        name="prepare",
    )(roots, packed, *map(placed, col_blocks))
    return pl.pallas_call(
        lambda *refs: kernel(n_tiles, order, *refs),
        out_shape=jax.ShapeDtypeStruct((n_tiles, block, block), jnp.float32),
        in_specs=[vmem] * (4 + n_row),
        out_specs=vmem,
        name="tiles",
    )(*map(placed, made), placed(own), *map(placed, row_blocks[1:]))


def solution(mesh):
    in_specs = (P(("row", "col"), None, None), P())
    out_specs = P(None, "row", "col")
    return jax.shard_map(local, mesh=mesh, in_specs=in_specs, out_specs=out_specs, check_vma=False)
```

```python
import math

import jax
import jax.numpy as jnp
import numpy as np
from jax import lax
from jax.experimental import pallas as pl
from jax.experimental.pallas import tpu as pltpu
from jax.sharding import PartitionSpec as P

WIDTH = 32
LANES = 128
DEPTH = 4

weight_var = 2.0
bias_var = 0.1


def remainder_coefficients(degree=6, nodes=64):
    u = 0.5 + 0.5 * np.cos(np.pi * (np.arange(nodes) + 0.5) / nodes)
    angle = 2.0 * np.arcsin(np.sqrt(0.5 * u))
    series = sum(
        (-1) ** n * 2.0 * n / math.factorial(2 * n + 1) * angle ** (2 * n + 1) * -1.0
        for n in range(1, 8)
    )
    exact = np.sin(angle) - angle * np.cos(angle)
    q = np.where(angle < 0.5, series, exact) / u**1.5
    fit = np.polynomial.chebyshev.Chebyshev.fit(u, q, degree, domain=[0.0, 1.0])
    return fit.convert(kind=np.polynomial.Polynomial).coef


COEFS = [float(v) / (2.0 * math.pi) for v in remainder_coefficients()]


class Stencil:
    def __init__(self, rows, block):
        self.rows, self.block = rows, block
        sub = lax.broadcasted_iota(jnp.int32, (rows, LANES), 0)
        lane = lax.broadcasted_iota(jnp.int32, (rows, LANES), 1)
        self.not_left = (lane % WIDTH) != 0
        self.not_right = (lane % WIDTH) != WIDTH - 1
        self.first_band = lane < WIDTH
        self.last_band = lane >= LANES - WIDTH
        self.above_inside = jnp.logical_and(self.first_band, sub >= block)
        self.below_inside = jnp.logical_and(self.last_band, sub < rows - block)
        self.even = (sub % 2) == 0
        self.sub, self.lane = sub, lane

    def box(self, m):
        left = jnp.where(self.not_left, pltpu.roll(m, 1, 1), 0.0)
        right = jnp.where(self.not_right, pltpu.roll(m, LANES - 1, 1), 0.0)
        across = m + left + right
        down = pltpu.roll(across, WIDTH, 1)
        up = pltpu.roll(across, LANES - WIDTH, 1)
        down_far = jnp.where(self.above_inside, pltpu.roll(down, self.block, 0), 0.0)
        up_far = jnp.where(self.below_inside, pltpu.roll(up, self.rows - self.block, 0), 0.0)
        return across + jnp.where(self.first_band, down_far, down) + jnp.where(self.last_band, up_far, up)

    def swapped(self, m):
        return jnp.where(self.even, pltpu.roll(m, self.rows - 1, 0), pltpu.roll(m, 1, 0))

    def channels(self, value):
        return [value[c * self.rows:(c + 1) * self.rows] for c in range(3)]

    def self_maps(self, value):
        energy = sum(v * v for v in self.channels(value))
        level = weight_var / 27.0 * self.box(energy) + bias_var
        levels = [level]
        for _ in range(DEPTH - 1):
            level = self.box(weight_var / 18.0 * level) + bias_var
            levels.append(level)
        inverse = [lax.rsqrt(v) for v in levels]
        return [v * r for v, r in zip(levels, inverse)], inverse


def prepare(powers, n_row, roots_ref, own_ref, near_ref, far_ref, own_out, pick_out, near_out, far_out, std_out, inv_out):
    n_tiles = roots_ref.shape[0]
    row_index, col_index = lax.axis_index("row"), lax.axis_index("col")
    block = own_ref.shape[0] // 24
    st = Stencil(8 * block, block)
    own_out[...] = own_ref[...]
    near_out[...] = near_ref[...]
    for s in range(n_tiles):
        root = roots_ref[s, col_index]
        source = root ^ row_index if powers else lax.rem(row_index - root + n_row, n_row)
        pick_out[s] = jnp.full((8, LANES), source, jnp.int32)
    pick_out[n_tiles] = jnp.full((8, LANES), lax.rem(col_index, 2), jnp.int32)
    value = far_ref[...]
    std, inv = st.self_maps(value)
    for d in range(2):
        turn = st.swapped if d else lambda v: v
        for c, v in enumerate(st.channels(value)):
            far_out[d, c] = turn(v)
        for l in range(DEPTH):
            std_out[d, l] = turn(std[l])
            inv_out[d, l] = turn(inv[l])


def kernel(n_tiles, order, pick_ref, near_ref, far_ref, std_ref, inv_ref, passed_ref, *refs):
    row_refs, out_ref = refs[:-1], refs[-1]
    block = row_refs[0].shape[0] // 24
    st = Stencil(8 * block, block)

    def chosen(flags, first, second):
        first, second = first.reshape(-1, 8, LANES), second.reshape(-1, 8, LANES)
        return jnp.where(flags[None], first, second).reshape(-1, LANES)

    odd = pick_ref[n_tiles] == 1
    near = chosen(odd, near_ref[...], passed_ref[...])
    near_std, near_inv = st.self_maps(near)
    columns = [
        [(st.channels(near), near_std, near_inv)] + [tuple([st.swapped(v) for v in part] for part in (st.channels(near), near_std, near_inv))],
        [([far_ref[d, c] for c in range(3)], [std_ref[d, l] for l in range(DEPTH)], [inv_ref[d, l] for l in range(DEPTH)]) for d in range(2)],
    ]

    def relu_map(k, scale, inverse):
        c = k * inverse
        u = jnp.maximum(1.0 - jnp.abs(c), 0.0)
        poly = jnp.full_like(u, COEFS[-1])
        for coef in COEFS[-2::-1]:
            poly = poly * u + coef
        return 0.5 * jnp.maximum(k, 0.0) + scale * (u * jnp.sqrt(u)) * poly

    sums = []
    for s in range(n_tiles):
        source = pick_ref[s]
        row_value = row_refs[0][...]
        for n, k in enumerate(order, 1):
            row_value = chosen(source == k, row_refs[n][...], row_value)
        row_std, row_inv = st.self_maps(row_value)
        for d in range(2):
            images, col_std, col_inv = columns[s][d]
            cross = sum(a * b for a, b in zip(st.channels(row_value), images))
            level = weight_var / 27.0 * st.box(cross) + bias_var
            for l in range(DEPTH):
                mapped = relu_map(level, row_std[l] * col_std[l], row_inv[l] * col_inv[l])
                if l < DEPTH - 1:
                    level = weight_var / 9.0 * st.box(mapped) + bias_var
            total = mapped[:8] + mapped[8:]
            total = total + pltpu.roll(total, 4, 0)
            sums.append(total + pltpu.roll(total, 2, 0))
    sub8 = st.sub[:8]
    packed = sums[0]
    for q in range(8):
        s, a, b = (q // 2) % 2, q % 2, q // 4
        packed = jnp.where(sub8 == q, sums[2 * s + (a ^ b)], packed)
    mean = jnp.sum(packed, axis=1, keepdims=True) * (1.0 / 1024.0)
    value = jnp.broadcast_to(weight_var * mean + bias_var, (8, LANES))
    result = jnp.where(st.lane[:8] == 0, value, pltpu.roll(value, 4, 0))
    for s in range(n_tiles):
        out_ref[s] = result[2 * s:2 * s + 2, 0:2]


def local(images, roots):
    n_row, n_col = lax.axis_size("row"), lax.axis_size("col")
    n_tiles = roots.shape[0]
    block, ch, pix = images.shape
    tiles = pix // LANES
    packed = images.reshape(block, ch, tiles, LANES).transpose(1, 2, 0, 3).reshape(ch * tiles * block, LANES)
    powers = n_row & (n_row - 1) == 0
    def moved(value, shift):
        pairs = []
        for i in range(n_row):
            for j in range(n_col):
                row, col = shift(i, j)
                pairs.append((i * n_col + j, row * n_col + col))
        return lax.ppermute(value, ("row", "col"), pairs)

    def row_shift(k, crossed):
        def shift(i, j):
            return (i ^ k if powers else (i + k) % n_row), (j ^ 1 if crossed else j)
        return shift

    near = moved(packed, lambda i, j: (i, j ^ 1))
    far = moved(packed, lambda i, j: (i, (j + 2) % n_col))
    order = [k for k in range(n_row - 1, 0, -1) if k % 2 == 0] + [k for k in range(n_row - 1, 0, -1) if k % 2]
    row_blocks = []
    for k in order:
        crossed = k % 2 == 1
        row_blocks.append(moved(near if crossed else packed, row_shift(k, crossed)))
    passed = moved(far, lambda i, j: (i, j ^ 1))
    vmem = pl.BlockSpec(memory_space=pltpu.VMEM)
    rows = 8 * block

    def placed(value):
        return pltpu.with_memory_space_constraint(value, pltpu.VMEM)

    own, pick, near_copy, *made = pl.pallas_call(
        lambda *refs: prepare(powers, n_row, *refs),
        out_shape=[
            pltpu.VMEM(packed.shape, jnp.float32),
            pltpu.VMEM((n_tiles + 1, 8, LANES), jnp.int32),
            pltpu.VMEM(packed.shape, jnp.float32),
            pltpu.VMEM((2, ch, rows, LANES), jnp.float32),
            pltpu.VMEM((2, DEPTH, rows, LANES), jnp.float32),
            pltpu.VMEM((2, DEPTH, rows, LANES), jnp.float32),
        ],
        in_specs=[pl.BlockSpec(memory_space=pltpu.SMEM)] + [vmem] * 3,
        out_specs=[vmem] * 6,
        name="prepare",
    )(roots, packed, placed(near), placed(far))
    return pl.pallas_call(
        lambda *refs: kernel(n_tiles, order, *refs),
        out_shape=jax.ShapeDtypeStruct((n_tiles, block, block), jnp.float32),
        in_specs=[vmem] * (7 + n_row - 1),
        out_specs=vmem,
        name="tiles",
    )(*map(placed, [pick, near_copy, *made, passed, own, *row_blocks]))


def solution(mesh):
    in_specs = (P(("row", "col"), None, None), P())
    out_specs = P(None, "row", "col")
    return jax.shard_map(local, mesh=mesh, in_specs=in_specs, out_specs=out_specs, check_vma=False)
```

```python
import math

import jax
import jax.numpy as jnp
import numpy as np
from jax import lax
from jax.experimental import pallas as pl
from jax.experimental.pallas import tpu as pltpu
from jax.sharding import PartitionSpec as P

WIDTH = 32
LANES = 128
DEPTH = 4

weight_var = 2.0
bias_var = 0.1


def remainder_coefficients(degree=6, nodes=64):
    u = 0.5 + 0.5 * np.cos(np.pi * (np.arange(nodes) + 0.5) / nodes)
    angle = 2.0 * np.arcsin(np.sqrt(0.5 * u))
    series = sum(
        (-1) ** n * 2.0 * n / math.factorial(2 * n + 1) * angle ** (2 * n + 1) * -1.0
        for n in range(1, 8)
    )
    exact = np.sin(angle) - angle * np.cos(angle)
    q = np.where(angle < 0.5, series, exact) / u**1.5
    fit = np.polynomial.chebyshev.Chebyshev.fit(u, q, degree, domain=[0.0, 1.0])
    return fit.convert(kind=np.polynomial.Polynomial).coef


COEFS = [float(v) / (2.0 * math.pi) for v in remainder_coefficients()]


def prepare(powers, n_row, roots_ref, own_ref, near_ref, far_ref, own_out, pick_out, near_out, far_out):
    n_tiles = roots_ref.shape[0]
    row_index, col_index = lax.axis_index("row"), lax.axis_index("col")
    own_out[...] = own_ref[...]
    near_out[...] = near_ref[...]
    far_out[...] = far_ref[...]
    for s in range(n_tiles):
        root = roots_ref[s, col_index]
        source = root ^ row_index if powers else lax.rem(row_index - root + n_row, n_row)
        pick_out[s] = jnp.full((8, LANES), source, jnp.int32)
    pick_out[n_tiles] = jnp.full((8, LANES), lax.rem(col_index, 2), jnp.int32)


def kernel(n_tiles, order, pick_ref, near_ref, far_ref, passed_ref, *refs):
    row_refs, out_ref = refs[:-1], refs[-1]
    block = row_refs[0].shape[0] // 24
    rows, bands = 8 * block, LANES // WIDTH
    sub = lax.broadcasted_iota(jnp.int32, (rows, LANES), 0)
    lane = lax.broadcasted_iota(jnp.int32, (rows, LANES), 1)
    not_left, not_right = (lane % WIDTH) != 0, (lane % WIDTH) != WIDTH - 1
    first_rows, last_rows = sub < block, sub >= rows - block
    even = (sub % 2) == 0
    group = lane // WIDTH
    other_image = (group % 2) == 1

    def box(maps):
        before = jnp.where(first_rows, 0.0, pltpu.roll(maps[-1], block, 0))
        after = jnp.where(last_rows, 0.0, pltpu.roll(maps[0], rows - block, 0))
        padded = [before] + maps + [after]
        sums = []
        for q in range(bands):
            down = padded[q] + padded[q + 1] + padded[q + 2]
            left = jnp.where(not_left, pltpu.roll(down, 1, 1), 0.0)
            right = jnp.where(not_right, pltpu.roll(down, LANES - 1, 1), 0.0)
            sums.append(down + left + right)
        return sums

    def swapped(m):
        return jnp.where(even, pltpu.roll(m, rows - 1, 0), pltpu.roll(m, 1, 0))

    def channels(value):
        return [value[c * rows:(c + 1) * rows] for c in range(3)]

    def regrouped(maps):
        turned = {}
        for b, m in enumerate(maps):
            for q in range(bands):
                shift = (b - q) % bands * WIDTH
                if (id(m), shift) not in turned:
                    turned[id(m), shift] = pltpu.roll(m, shift, 1) if shift else m
        out = []
        for q in range(bands):
            parts = [turned[id(m), (b - q) % bands * WIDTH] for b, m in enumerate(maps)]
            value = parts[-1]
            for b in range(bands - 2, -1, -1):
                value = jnp.where(group == b, parts[b], value)
            out.append(value)
        return out

    def self_maps(energy):
        levels = [[weight_var / 27.0 * v + bias_var for v in box(energy)]]
        for _ in range(DEPTH - 1):
            levels.append([weight_var / 18.0 * v + bias_var for v in box(levels[-1])])
        inverse = [[lax.rsqrt(v) for v in level] for level in levels]
        return [[v * r for v, r in zip(*pair)] for pair in zip(levels, inverse)], inverse

    def relu_map(k, scale, inverse, factor):
        u = jnp.maximum(1.0 - jnp.abs(k * inverse), 1e-30)
        u2 = u * u
        root = lax.rsqrt(u)
        a = [factor * v for v in COEFS]
        poly = (a[0] + a[1] * u) + (a[2] + a[3] * u) * u2 + ((a[4] + a[5] * u) + a[6] * u2) * (u2 * u2)
        return (0.5 * factor) * jnp.maximum(k, 0.0) + (scale * u2) * poly * root

    def chosen(flags, first, second):
        first, second = first.reshape(-1, 8, LANES), second.reshape(-1, 8, LANES)
        return jnp.where(flags[None], first, second).reshape(-1, LANES)

    odd = pick_ref[n_tiles] == 1
    cols = [channels(chosen(odd, near_ref[...], passed_ref[...])), channels(far_ref[...])]
    row_values = []
    for s in range(n_tiles):
        value = row_refs[0][...]
        for n, k in enumerate(order, 1):
            value = chosen(pick_ref[s] == k, row_refs[n][...], value)
        row_values.append(channels(value))

    def dot(first, second):
        return sum(a * b for a, b in zip(first, second))

    turned_cols = [[swapped(v) for v in col] for col in cols]
    cross = regrouped([dot(r, c) for s, r in enumerate(row_values) for c in (cols[s], turned_cols[s])])
    row_energy = [dot(r, r) for r in row_values]
    col_energy = [dot(c, c) for c in cols]
    row_std, row_inv = self_maps(regrouped([row_energy[0], row_energy[0], row_energy[1], row_energy[1]]))
    col_maps = regrouped([col_energy[0], col_energy[0], col_energy[1], col_energy[1]])
    col_std, col_inv = self_maps([jnp.where(other_image, swapped(m), m) for m in col_maps])

    levels = [weight_var / 27.0 * v + bias_var for v in box(cross)]
    for l in range(DEPTH):
        last = l == DEPTH - 1
        factor = weight_var / 1024.0 if last else weight_var / 9.0
        mapped = [
            relu_map(k, rs * cs, ri * ci, factor)
            for k, rs, cs, ri, ci in zip(levels, row_std[l], col_std[l], row_inv[l], col_inv[l])
        ]
        if not last:
            levels = [v + bias_var for v in box(mapped)]
    total = sum(mapped)
    total = total[:8] + total[8:]
    total = total + pltpu.roll(total, 4, 0)
    total = total + pltpu.roll(total, 2, 0)
    sub8 = sub[:8]
    a, s, b = sub8 % 2, sub8 // 2 % 2, sub8 // 4
    wanted = 2 * s + jnp.where(a == b, 0, 1)
    value = jnp.sum(jnp.where(group[:8] == wanted, total, 0.0), axis=1, keepdims=True) + bias_var
    value = jnp.broadcast_to(value, (8, LANES))
    result = jnp.where(lane[:8] == 0, value, pltpu.roll(value, 4, 0))
    for s in range(n_tiles):
        out_ref[s] = result[2 * s:2 * s + 2, 0:2]


def local(images, roots):
    n_row, n_col = lax.axis_size("row"), lax.axis_size("col")
    n_tiles = roots.shape[0]
    block, ch, pix = images.shape
    tiles = pix // LANES
    packed = images.reshape(block, ch, tiles, LANES).transpose(1, 2, 0, 3).reshape(ch * tiles * block, LANES)
    powers = n_row & (n_row - 1) == 0
    def moved(value, shift):
        pairs = []
        for i in range(n_row):
            for j in range(n_col):
                row, col = shift(i, j)
                pairs.append((i * n_col + j, row * n_col + col))
        return lax.ppermute(value, ("row", "col"), pairs)

    def row_shift(k, crossed):
        def shift(i, j):
            return (i ^ k if powers else (i + k) % n_row), (j ^ 1 if crossed else j)
        return shift

    near = moved(packed, lambda i, j: (i, j ^ 1))
    far = moved(packed, lambda i, j: (i, (j + 2) % n_col))
    order = [k for k in range(n_row - 1, 0, -1) if k % 2 == 0] + [k for k in range(n_row - 1, 0, -1) if k % 2]
    row_blocks = []
    for k in order:
        crossed = k % 2 == 1
        row_blocks.append(moved(near if crossed else packed, row_shift(k, crossed)))
    passed = moved(far, lambda i, j: (i, j ^ 1))
    vmem = pl.BlockSpec(memory_space=pltpu.VMEM)

    def placed(value):
        return pltpu.with_memory_space_constraint(value, pltpu.VMEM)

    own, pick, near_copy, far_copy = pl.pallas_call(
        lambda *refs: prepare(powers, n_row, *refs),
        out_shape=[pltpu.VMEM(packed.shape, jnp.float32), pltpu.VMEM((n_tiles + 1, 8, LANES), jnp.int32)] + [pltpu.VMEM(packed.shape, jnp.float32)] * 2,
        in_specs=[pl.BlockSpec(memory_space=pltpu.SMEM)] + [vmem] * 3,
        out_specs=[vmem] * 4,
        name="prepare",
    )(roots, packed, placed(near), placed(far))
    return pl.pallas_call(
        lambda *refs: kernel(n_tiles, order, *refs),
        out_shape=jax.ShapeDtypeStruct((n_tiles, block, block), jnp.float32),
        in_specs=[vmem] * (4 + n_row),
        out_specs=vmem,
        name="tiles",
    )(*map(placed, [pick, near_copy, far_copy, passed, own, *row_blocks]))


def solution(mesh):
    in_specs = (P(("row", "col"), None, None), P())
    out_specs = P(None, "row", "col")
    return jax.shard_map(local, mesh=mesh, in_specs=in_specs, out_specs=out_specs, check_vma=False)
```

```python
import math

import jax
import jax.numpy as jnp
import numpy as np
from jax import lax
from jax.experimental import pallas as pl
from jax.experimental.pallas import tpu as pltpu
from jax.sharding import PartitionSpec as P

WIDTH = 32
LANES = 128
DEPTH = 4

weight_var = 2.0
bias_var = 0.1


def remainder_coefficients(degree=6, nodes=64):
    u = 0.5 + 0.5 * np.cos(np.pi * (np.arange(nodes) + 0.5) / nodes)
    angle = 2.0 * np.arcsin(np.sqrt(0.5 * u))
    series = sum(
        (-1) ** n * 2.0 * n / math.factorial(2 * n + 1) * angle ** (2 * n + 1) * -1.0
        for n in range(1, 8)
    )
    exact = np.sin(angle) - angle * np.cos(angle)
    q = np.where(angle < 0.5, series, exact) / u**1.5
    fit = np.polynomial.chebyshev.Chebyshev.fit(u, q, degree, domain=[0.0, 1.0])
    return fit.convert(kind=np.polynomial.Polynomial).coef


COEFS = [float(v) / (2.0 * math.pi) for v in remainder_coefficients()]


def join(own_ref, near_ref, tile_ref, both_out):
    rows = own_ref.shape[0]
    both_out[pl.ds(0, rows)] = own_ref[...]
    both_out[pl.ds(rows, rows)] = near_ref[...]


def blank(out):
    out[...] = jnp.zeros(out.shape, out.dtype)


def relay(near_ref, near_out):
    near_out[...] = near_ref[...]


def first_half(both_ref, half_out):
    half_out[...] = both_ref[pl.ds(0, half_out.shape[0])]


def prepare(row_source, slots, roots_ref, far_ref, pick_out, far_out):
    n_tiles = roots_ref.shape[0]
    row_index, col_index = lax.axis_index("row"), lax.axis_index("col")
    odd = lax.rem(col_index, 2)
    far_out[...] = far_ref[...]
    for s in range(n_tiles):
        source = row_source(row_index, roots_ref[s, col_index])
        slot = jnp.int32(0)
        for n, (on_even, on_odd) in enumerate(slots, 1):
            slot = jnp.where(source == jnp.where(odd == 1, on_odd, on_even), n, slot)
        pick_out[s] = jnp.full((8, LANES), slot, jnp.int32)
    pick_out[n_tiles] = jnp.full((8, LANES), odd, jnp.int32)


def kernel(n_tiles, pick_ref, far_ref, passed_ref, both_ref, *refs):
    row_refs, out_ref = refs[:-1], refs[-1]
    block = far_ref.shape[0] // 24
    rows, bands = 8 * block, LANES // WIDTH
    sub = lax.broadcasted_iota(jnp.int32, (rows, LANES), 0)
    lane = lax.broadcasted_iota(jnp.int32, (rows, LANES), 1)
    not_left, not_right = (lane % WIDTH) != 0, (lane % WIDTH) != WIDTH - 1
    first_rows, last_rows = sub < block, sub >= rows - block
    even = (sub % 2) == 0
    group = lane // WIDTH
    other_image = (group % 2) == 1

    def box(maps):
        before = jnp.where(first_rows, 0.0, pltpu.roll(maps[-1], block, 0))
        after = jnp.where(last_rows, 0.0, pltpu.roll(maps[0], rows - block, 0))
        padded = [before] + maps + [after]
        sums = []
        for q in range(bands):
            down = padded[q] + padded[q + 1] + padded[q + 2]
            left = jnp.where(not_left, pltpu.roll(down, 1, 1), 0.0)
            right = jnp.where(not_right, pltpu.roll(down, LANES - 1, 1), 0.0)
            sums.append(down + left + right)
        return sums

    def swapped(m):
        return jnp.where(even, pltpu.roll(m, rows - 1, 0), pltpu.roll(m, 1, 0))

    def channels(value):
        return [value[c * rows:(c + 1) * rows] for c in range(3)]

    def regrouped(maps):
        turned = {}
        for b, m in enumerate(maps):
            for q in range(bands):
                shift = (b - q) % bands * WIDTH
                if (id(m), shift) not in turned:
                    turned[id(m), shift] = pltpu.roll(m, shift, 1) if shift else m
        out = []
        for q in range(bands):
            parts = [turned[id(m), (b - q) % bands * WIDTH] for b, m in enumerate(maps)]
            value = parts[-1]
            for b in range(bands - 2, -1, -1):
                value = jnp.where(group == b, parts[b], value)
            out.append(value)
        return out

    def self_maps(energy):
        levels = [[weight_var / 27.0 * v + bias_var for v in box(energy)]]
        for _ in range(DEPTH - 1):
            levels.append([weight_var / 18.0 * v + bias_var for v in box(levels[-1])])
        inverse = [[lax.rsqrt(v) for v in level] for level in levels]
        return [[v * r for v, r in zip(*pair)] for pair in zip(levels, inverse)], inverse

    def relu_map(k, scale, inverse, factor):
        u = jnp.maximum(1.0 - jnp.abs(k * inverse), 1e-30)
        u2 = u * u
        root = lax.rsqrt(u)
        a = [factor * v for v in COEFS]
        poly = (a[0] + a[1] * u) + (a[2] + a[3] * u) * u2 + ((a[4] + a[5] * u) + a[6] * u2) * (u2 * u2)
        return (0.5 * factor) * jnp.maximum(k, 0.0) + (scale * u2) * poly * root

    def chosen(flags, first, second):
        first, second = first.reshape(-1, 8, LANES), second.reshape(-1, 8, LANES)
        return jnp.where(flags[None], first, second).reshape(-1, LANES)

    odd = pick_ref[n_tiles] == 1
    cols = [channels(chosen(odd, both_ref[pl.ds(3 * rows, 3 * rows)], passed_ref[...])), channels(far_ref[...])]
    row_values = []
    for s in range(n_tiles):
        value = both_ref[pl.ds(0, 3 * rows)]
        for n, ref in enumerate(row_refs, 1):
            value = chosen(pick_ref[s] == n, ref[pl.ds(ref.shape[0] - 3 * rows, 3 * rows)], value)
        row_values.append(channels(value))

    def dot(first, second):
        return sum(a * b for a, b in zip(first, second))

    turned_cols = [[swapped(v) for v in col] for col in cols]
    cross = regrouped([dot(r, c) for s, r in enumerate(row_values) for c in (cols[s], turned_cols[s])])
    row_energy = [dot(r, r) for r in row_values]
    col_energy = [dot(c, c) for c in cols]
    row_std, row_inv = self_maps(regrouped([row_energy[0], row_energy[0], row_energy[1], row_energy[1]]))
    col_maps = regrouped([col_energy[0], col_energy[0], col_energy[1], col_energy[1]])
    col_std, col_inv = self_maps([jnp.where(other_image, swapped(m), m) for m in col_maps])

    levels = [weight_var / 27.0 * v + bias_var for v in box(cross)]
    for l in range(DEPTH):
        last = l == DEPTH - 1
        factor = weight_var / 1024.0 if last else weight_var / 9.0
        mapped = [
            relu_map(k, rs * cs, ri * ci, factor)
            for k, rs, cs, ri, ci in zip(levels, row_std[l], col_std[l], row_inv[l], col_inv[l])
        ]
        if not last:
            levels = [v + bias_var for v in box(mapped)]
    total = sum(mapped)
    total = total[:8] + total[8:]
    total = total + pltpu.roll(total, 4, 0)
    total = total + pltpu.roll(total, 2, 0)
    sub8 = sub[:8]
    a, s, b = sub8 % 2, sub8 // 2 % 2, sub8 // 4
    wanted = 2 * s + jnp.where(a == b, 0, 1)
    value = jnp.sum(jnp.where(group[:8] == wanted, total, 0.0), axis=1, keepdims=True) + bias_var
    value = jnp.broadcast_to(value, (8, LANES))
    result = jnp.where(lane[:8] == 0, value, pltpu.roll(value, 4, 0))
    for s in range(n_tiles):
        out_ref[s] = result[2 * s:2 * s + 2, 0:2]


def local(images, roots):
    n_row, n_col = lax.axis_size("row"), lax.axis_size("col")
    n_tiles = roots.shape[0]
    block, ch, pix = images.shape
    tiles = pix // LANES
    packed = images.reshape(block, ch, tiles, LANES).transpose(1, 2, 0, 3).reshape(ch * tiles * block, LANES)
    powers = n_row & (n_row - 1) == 0

    def row_target(i, k):
        return i ^ k if powers else (i + k) % n_row

    def row_source(row_index, root):
        return root ^ row_index if powers else lax.rem(row_index - root + n_row, n_row)

    def moved(value, target):
        pairs = []
        for i in range(n_row):
            for j in range(n_col):
                row, col = target(i, j)
                pairs.append((i * n_col + j, row * n_col + col))
        return lax.ppermute(value, ("row", "col"), pairs)

    def placed(value):
        return pltpu.with_memory_space_constraint(value, pltpu.VMEM)

    vmem = pl.BlockSpec(memory_space=pltpu.VMEM)
    single = pltpu.VMEM(packed.shape, jnp.float32)
    double = pltpu.VMEM((2 * packed.shape[0], LANES), jnp.float32)

    def on_core(body, out_shape, *values, flops=0):
        return pl.pallas_call(
            body, out_shape=out_shape, in_specs=[vmem] * len(values), out_specs=vmem, name=body.__name__,
            cost_estimate=pl.CostEstimate(flops=flops, bytes_accessed=0, transcendentals=0),
        )(*map(placed, values))

    near = moved(packed, lambda i, j: (i, j ^ 1))
    tile = on_core(blank, pltpu.VMEM((8, LANES), jnp.float32), flops=3000000)
    ahead, tile = lax.optimization_barrier((packed, tile))
    far = moved(ahead, lambda i, j: (i, (j + 2) % n_col))
    both = on_core(join, double, packed, on_core(relay, single, near, flops=3000000), tile)
    row_blocks, slots = [], []
    for k in range(1, n_row - 1, 2):
        pair = moved(both, lambda i, j, k=k: (row_target(i, k + 1 if j % 2 == 0 else k), j ^ 1))
        swapped = moved(on_core(first_half, single, pair), lambda i, j: (i, j ^ 1))
        row_blocks += [pair, swapped]
        slots += [(k, k + 1), (k + 1, k)]
    if n_row % 2 == 0:
        row_blocks.append(moved(on_core(relay, single, near, flops=20_000_000_000), lambda i, j: (row_target(i, n_row - 1), j ^ 1)))
        slots.append((n_row - 1, n_row - 1))
    passed = moved(far, lambda i, j: (i, j ^ 1))
    pick, far_copy = pl.pallas_call(
        lambda *refs: prepare(row_source, slots, *refs),
        out_shape=[pltpu.VMEM((n_tiles + 1, 8, LANES), jnp.int32), single],
        in_specs=[pl.BlockSpec(memory_space=pltpu.SMEM), vmem],
        out_specs=[vmem] * 2,
        name="prepare",
    )(roots, placed(far))
    return pl.pallas_call(
        lambda *refs: kernel(n_tiles, *refs),
        out_shape=jax.ShapeDtypeStruct((n_tiles, block, block), jnp.float32),
        in_specs=[vmem] * (4 + len(row_blocks)),
        out_specs=vmem,
        name="tiles",
    )(*map(placed, [pick, far_copy, passed, both, *row_blocks]))


def solution(mesh):
    in_specs = (P(("row", "col"), None, None), P())
    out_specs = P(None, "row", "col")
    return jax.shard_map(local, mesh=mesh, in_specs=in_specs, out_specs=out_specs, check_vma=False)
```

```python
import math

import jax
import jax.numpy as jnp
import numpy as np
from jax import lax
from jax.experimental import pallas as pl
from jax.experimental.pallas import tpu as pltpu
from jax.sharding import PartitionSpec as P

WIDTH = 32
LANES = 128
DEPTH = 4

weight_var = 2.0
bias_var = 0.1


def remainder_coefficients(degree=6, nodes=64):
    u = 0.5 + 0.5 * np.cos(np.pi * (np.arange(nodes) + 0.5) / nodes)
    angle = 2.0 * np.arcsin(np.sqrt(0.5 * u))
    series = sum(
        (-1) ** n * 2.0 * n / math.factorial(2 * n + 1) * angle ** (2 * n + 1) * -1.0
        for n in range(1, 8)
    )
    exact = np.sin(angle) - angle * np.cos(angle)
    q = np.where(angle < 0.5, series, exact) / u**1.5
    fit = np.polynomial.chebyshev.Chebyshev.fit(u, q, degree, domain=[0.0, 1.0])
    return fit.convert(kind=np.polynomial.Polynomial).coef


COEFS = [float(v) / (2.0 * math.pi) for v in remainder_coefficients()]


def join(own_ref, near_ref, tile_ref, both_out):
    rows = own_ref.shape[0]
    both_out[pl.ds(0, rows)] = own_ref[...]
    both_out[pl.ds(rows, rows)] = near_ref[...]


def blank(out):
    out[...] = jnp.zeros(out.shape, out.dtype)


def relay(near_ref, near_out):
    near_out[...] = near_ref[...]


def first_half(both_ref, half_out):
    half_out[...] = both_ref[pl.ds(0, half_out.shape[0])]


def prepare(row_source, slots, roots_ref, pick_out):
    n_tiles = roots_ref.shape[0]
    row_index, col_index = lax.axis_index("row"), lax.axis_index("col")
    odd = lax.rem(col_index, 2)
    for s in range(n_tiles):
        source = row_source(row_index, roots_ref[s, col_index])
        slot = jnp.int32(0)
        for n, (on_even, on_odd) in enumerate(slots, 1):
            slot = jnp.where(source == jnp.where(odd == 1, on_odd, on_even), n, slot)
        pick_out[s] = jnp.full((8, LANES), slot, jnp.int32)
    pick_out[n_tiles] = jnp.full((8, LANES), odd, jnp.int32)


def kernel(n_tiles, pick_ref, far_ref, passed_ref, both_ref, *refs):
    row_refs, out_ref = refs[:-1], refs[-1]
    block = far_ref.shape[0] // 24
    rows, bands = 8 * block, LANES // WIDTH
    sub = lax.broadcasted_iota(jnp.int32, (rows, LANES), 0)
    lane = lax.broadcasted_iota(jnp.int32, (rows, LANES), 1)
    not_left, not_right = (lane % WIDTH) != 0, (lane % WIDTH) != WIDTH - 1
    first_rows, last_rows = sub < block, sub >= rows - block
    even = (sub % 2) == 0
    group = lane // WIDTH
    other_image = (group % 2) == 1

    def box(maps):
        before = jnp.where(first_rows, 0.0, pltpu.roll(maps[-1], block, 0))
        after = jnp.where(last_rows, 0.0, pltpu.roll(maps[0], rows - block, 0))
        padded = [before] + maps + [after]
        sums = []
        for q in range(bands):
            down = padded[q] + padded[q + 1] + padded[q + 2]
            left = jnp.where(not_left, pltpu.roll(down, 1, 1), 0.0)
            right = jnp.where(not_right, pltpu.roll(down, LANES - 1, 1), 0.0)
            sums.append(down + left + right)
        return sums

    def swapped(m):
        return jnp.where(even, pltpu.roll(m, rows - 1, 0), pltpu.roll(m, 1, 0))

    def channels(value):
        return [value[c * rows:(c + 1) * rows] for c in range(3)]

    def regrouped(maps):
        turned = {}
        for b, m in enumerate(maps):
            for q in range(bands):
                shift = (b - q) % bands * WIDTH
                if (id(m), shift) not in turned:
                    turned[id(m), shift] = pltpu.roll(m, shift, 1) if shift else m
        out = []
        for q in range(bands):
            parts = [turned[id(m), (b - q) % bands * WIDTH] for b, m in enumerate(maps)]
            value = parts[-1]
            for b in range(bands - 2, -1, -1):
                value = jnp.where(group == b, parts[b], value)
            out.append(value)
        return out

    def self_maps(energy):
        levels = [[weight_var / 27.0 * v + bias_var for v in box(energy)]]
        for _ in range(DEPTH - 1):
            levels.append([weight_var / 18.0 * v + bias_var for v in box(levels[-1])])
        inverse = [[lax.rsqrt(v) for v in level] for level in levels]
        return [[v * r for v, r in zip(*pair)] for pair in zip(levels, inverse)], inverse

    def relu_map(k, scale, inverse, factor):
        u = jnp.maximum(1.0 - jnp.abs(k * inverse), 1e-30)
        u2 = u * u
        root = lax.rsqrt(u)
        a = [factor * v for v in COEFS]
        poly = (a[0] + a[1] * u) + (a[2] + a[3] * u) * u2 + ((a[4] + a[5] * u) + a[6] * u2) * (u2 * u2)
        return (0.5 * factor) * jnp.maximum(k, 0.0) + (scale * u2) * poly * root

    def chosen(flags, first, second):
        first, second = first.reshape(-1, 8, LANES), second.reshape(-1, 8, LANES)
        return jnp.where(flags[None], first, second).reshape(-1, LANES)

    odd = pick_ref[n_tiles] == 1
    cols = [channels(chosen(odd, both_ref[pl.ds(3 * rows, 3 * rows)], far_ref[...])), channels(passed_ref[...])]
    row_values = []
    for s in range(n_tiles):
        value = both_ref[pl.ds(0, 3 * rows)]
        for n, ref in enumerate(row_refs, 1):
            value = chosen(pick_ref[s] == n, ref[pl.ds(ref.shape[0] - 3 * rows, 3 * rows)], value)
        row_values.append(channels(value))

    def dot(first, second):
        return sum(a * b for a, b in zip(first, second))

    turned_cols = [[swapped(v) for v in col] for col in cols]
    cross = regrouped([dot(r, c) for s, r in enumerate(row_values) for c in (cols[s], turned_cols[s])])
    row_energy = [dot(r, r) for r in row_values]
    col_energy = [dot(c, c) for c in cols]
    row_std, row_inv = self_maps(regrouped([row_energy[0], row_energy[0], row_energy[1], row_energy[1]]))
    col_maps = regrouped([col_energy[0], col_energy[0], col_energy[1], col_energy[1]])
    col_std, col_inv = self_maps([jnp.where(other_image, swapped(m), m) for m in col_maps])

    levels = [weight_var / 27.0 * v + bias_var for v in box(cross)]
    for l in range(DEPTH):
        last = l == DEPTH - 1
        factor = weight_var / 1024.0 if last else weight_var / 9.0
        mapped = [
            relu_map(k, rs * cs, ri * ci, factor)
            for k, rs, cs, ri, ci in zip(levels, row_std[l], col_std[l], row_inv[l], col_inv[l])
        ]
        if not last:
            levels = [v + bias_var for v in box(mapped)]
    total = sum(mapped)
    total = total[:8] + total[8:]
    total = total + pltpu.roll(total, 4, 0)
    total = total + pltpu.roll(total, 2, 0)
    sub8 = sub[:8]
    a, s, b = sub8 % 2, sub8 // 2 % 2, sub8 // 4
    wanted = 2 * s + jnp.where(a == b, 0, 1)
    value = jnp.sum(jnp.where(group[:8] == wanted, total, 0.0), axis=1, keepdims=True) + bias_var
    value = jnp.broadcast_to(value, (8, LANES))
    result = jnp.where(lane[:8] == 0, value, pltpu.roll(value, 4, 0))
    for s in range(n_tiles):
        out_ref[s] = result[2 * s:2 * s + 2, 0:2]


def local(images, roots):
    n_row, n_col = lax.axis_size("row"), lax.axis_size("col")
    n_tiles = roots.shape[0]
    block, ch, pix = images.shape
    tiles = pix // LANES
    packed = images.reshape(block, ch, tiles, LANES).transpose(1, 2, 0, 3).reshape(ch * tiles * block, LANES)
    powers = n_row & (n_row - 1) == 0

    def row_target(i, k):
        return i ^ k if powers else (i + k) % n_row

    def row_source(row_index, root):
        return root ^ row_index if powers else lax.rem(row_index - root + n_row, n_row)

    def moved(value, target):
        pairs = []
        for i in range(n_row):
            for j in range(n_col):
                row, col = target(i, j)
                pairs.append((i * n_col + j, row * n_col + col))
        return lax.ppermute(value, ("row", "col"), pairs)

    def placed(value):
        return pltpu.with_memory_space_constraint(value, pltpu.VMEM)

    vmem = pl.BlockSpec(memory_space=pltpu.VMEM)
    single = pltpu.VMEM(packed.shape, jnp.float32)
    double = pltpu.VMEM((2 * packed.shape[0], LANES), jnp.float32)

    def on_core(body, out_shape, *values, flops=0):
        return pl.pallas_call(
            body, out_shape=out_shape, in_specs=[vmem] * len(values), out_specs=vmem, name=body.__name__,
            cost_estimate=pl.CostEstimate(flops=flops, bytes_accessed=0, transcendentals=0),
        )(*map(placed, values))

    near = moved(packed, lambda i, j: (i, j ^ 1))
    tile = on_core(blank, pltpu.VMEM((8, LANES), jnp.float32), flops=3000000)
    ahead, tile = lax.optimization_barrier((packed, tile))
    far = moved(ahead, lambda i, j: (i, ((j + 2) % n_col) ^ 1))
    both = on_core(join, double, packed, on_core(relay, single, near, flops=3000000), tile)
    row_blocks, slots = [], []
    for k in range(1, n_row - 1, 2):
        pair = moved(both, lambda i, j, k=k: (row_target(i, k + 1 if j % 2 == 0 else k), j ^ 1))
        swapped = moved(on_core(first_half, single, pair), lambda i, j: (i, j ^ 1))
        row_blocks += [pair, swapped]
        slots += [(k, k + 1), (k + 1, k)]
    if n_row % 2 == 0:
        row_blocks.append(moved(on_core(relay, single, near, flops=20_000_000_000), lambda i, j: (row_target(i, n_row - 1), j ^ 1)))
        slots.append((n_row - 1, n_row - 1))
    passed = moved(far, lambda i, j: (i, j ^ 1))
    pick = pl.pallas_call(
        lambda *refs: prepare(row_source, slots, *refs),
        out_shape=pltpu.VMEM((n_tiles + 1, 8, LANES), jnp.int32),
        in_specs=[pl.BlockSpec(memory_space=pltpu.SMEM)],
        out_specs=vmem,
        name="prepare",
    )(roots)
    return pl.pallas_call(
        lambda *refs: kernel(n_tiles, *refs),
        out_shape=jax.ShapeDtypeStruct((n_tiles, block, block), jnp.float32),
        in_specs=[vmem] * (4 + len(row_blocks)),
        out_specs=vmem,
        name="tiles",
    )(*map(placed, [pick, far, passed, both, *row_blocks]))


def solution(mesh):
    in_specs = (P(("row", "col"), None, None), P())
    out_specs = P(None, "row", "col")
    return jax.shard_map(local, mesh=mesh, in_specs=in_specs, out_specs=out_specs, check_vma=False)
```

```python
import math

import jax
import jax.numpy as jnp
import numpy as np
from jax import lax
from jax.experimental import pallas as pl
from jax.experimental.pallas import tpu as pltpu
from jax.sharding import PartitionSpec as P

WIDTH = 32
LANES = 128
DEPTH = 4

weight_var = 2.0
bias_var = 0.1


def remainder_coefficients(degree=6, nodes=64):
    u = 0.5 + 0.5 * np.cos(np.pi * (np.arange(nodes) + 0.5) / nodes)
    angle = 2.0 * np.arcsin(np.sqrt(0.5 * u))
    series = sum(
        (-1) ** n * 2.0 * n / math.factorial(2 * n + 1) * angle ** (2 * n + 1) * -1.0
        for n in range(1, 8)
    )
    exact = np.sin(angle) - angle * np.cos(angle)
    q = np.where(angle < 0.5, series, exact) / u**1.5
    fit = np.polynomial.chebyshev.Chebyshev.fit(u, q, degree, domain=[0.0, 1.0])
    return fit.convert(kind=np.polynomial.Polynomial).coef


COEFS = [float(v) / (2.0 * math.pi) for v in remainder_coefficients()]


def join(own_ref, near_ref, tile_ref, both_out):
    rows = own_ref.shape[0]
    both_out[pl.ds(0, rows)] = own_ref[...]
    both_out[pl.ds(rows, rows)] = near_ref[...]


def blank(out):
    out[...] = jnp.zeros(out.shape, out.dtype)


def relay(near_ref, near_out):
    near_out[...] = near_ref[...]


def handed(far_ref, *refs):
    pair_refs, out = refs[:-1], refs[-1]
    rows = far_ref.shape[0]
    out[pl.ds(0, rows)] = far_ref[...]
    for n, ref in enumerate(pair_refs, 1):
        out[pl.ds(n * rows, rows)] = ref[pl.ds(0, rows)]


def prepare(row_source, slots, roots_ref, pick_out):
    n_tiles = roots_ref.shape[0]
    row_index, col_index = lax.axis_index("row"), lax.axis_index("col")
    odd = lax.rem(col_index, 2)
    for s in range(n_tiles):
        source = row_source(row_index, roots_ref[s, col_index])
        slot = jnp.int32(0)
        for n, (on_even, on_odd) in enumerate(slots, 1):
            slot = jnp.where(source == jnp.where(odd == 1, on_odd, on_even), n, slot)
        pick_out[s] = jnp.full((8, LANES), slot, jnp.int32)
    pick_out[n_tiles] = jnp.full((8, LANES), odd, jnp.int32)


def kernel(n_tiles, pick_ref, far_ref, passed_ref, both_ref, *refs):
    row_refs, out_ref = refs[:-1], refs[-1]
    block = far_ref.shape[0] // 24
    rows, bands = 8 * block, LANES // WIDTH
    sub = lax.broadcasted_iota(jnp.int32, (rows, LANES), 0)
    lane = lax.broadcasted_iota(jnp.int32, (rows, LANES), 1)
    not_left, not_right = (lane % WIDTH) != 0, (lane % WIDTH) != WIDTH - 1
    first_rows, last_rows = sub < block, sub >= rows - block
    even = (sub % 2) == 0
    group = lane // WIDTH
    other_image = (group % 2) == 1

    def box(maps):
        before = jnp.where(first_rows, 0.0, pltpu.roll(maps[-1], block, 0))
        after = jnp.where(last_rows, 0.0, pltpu.roll(maps[0], rows - block, 0))
        padded = [before] + maps + [after]
        sums = []
        for q in range(bands):
            down = padded[q] + padded[q + 1] + padded[q + 2]
            left = jnp.where(not_left, pltpu.roll(down, 1, 1), 0.0)
            right = jnp.where(not_right, pltpu.roll(down, LANES - 1, 1), 0.0)
            sums.append(down + left + right)
        return sums

    def swapped(m):
        return jnp.where(even, pltpu.roll(m, rows - 1, 0), pltpu.roll(m, 1, 0))

    def channels(value):
        return [value[c * rows:(c + 1) * rows] for c in range(3)]

    def regrouped(maps):
        turned = {}
        for b, m in enumerate(maps):
            for q in range(bands):
                shift = (b - q) % bands * WIDTH
                if (id(m), shift) not in turned:
                    turned[id(m), shift] = pltpu.roll(m, shift, 1) if shift else m
        out = []
        for q in range(bands):
            parts = [turned[id(m), (b - q) % bands * WIDTH] for b, m in enumerate(maps)]
            value = parts[-1]
            for b in range(bands - 2, -1, -1):
                value = jnp.where(group == b, parts[b], value)
            out.append(value)
        return out

    def self_maps(energy):
        levels = [[weight_var / 27.0 * v + bias_var for v in box(energy)]]
        for _ in range(DEPTH - 1):
            levels.append([weight_var / 18.0 * v + bias_var for v in box(levels[-1])])
        inverse = [[lax.rsqrt(v) for v in level] for level in levels]
        return [[v * r for v, r in zip(*pair)] for pair in zip(levels, inverse)], inverse

    def relu_map(k, scale, inverse, factor):
        u = jnp.maximum(1.0 - jnp.abs(k * inverse), 1e-30)
        u2 = u * u
        root = lax.rsqrt(u)
        a = [factor * v for v in COEFS]
        poly = (a[0] + a[1] * u) + (a[2] + a[3] * u) * u2 + ((a[4] + a[5] * u) + a[6] * u2) * (u2 * u2)
        return (0.5 * factor) * jnp.maximum(k, 0.0) + (scale * u2) * poly * root

    def chosen(flags, first, second):
        first, second = first.reshape(-1, 8, LANES), second.reshape(-1, 8, LANES)
        return jnp.where(flags[None], first, second).reshape(-1, LANES)

    odd = pick_ref[n_tiles] == 1
    cols = [channels(chosen(odd, both_ref[pl.ds(3 * rows, 3 * rows)], far_ref[...])), channels(passed_ref[pl.ds(0, 3 * rows)])]
    row_blocks = []
    for n in range(passed_ref.shape[0] // (3 * rows) - 1):
        row_blocks += [(row_refs[n], 3 * rows), (passed_ref, (n + 1) * 3 * rows)]
    row_blocks += [(ref, 0) for ref in row_refs[len(row_blocks) // 2:]]
    row_values = []
    for s in range(n_tiles):
        value = both_ref[pl.ds(0, 3 * rows)]
        for n, (ref, at) in enumerate(row_blocks, 1):
            value = chosen(pick_ref[s] == n, ref[pl.ds(at, 3 * rows)], value)
        row_values.append(channels(value))

    def dot(first, second):
        return sum(a * b for a, b in zip(first, second))

    turned_cols = [[swapped(v) for v in col] for col in cols]
    cross = regrouped([dot(r, c) for s, r in enumerate(row_values) for c in (cols[s], turned_cols[s])])
    row_energy = [dot(r, r) for r in row_values]
    col_energy = [dot(c, c) for c in cols]
    row_std, row_inv = self_maps(regrouped([row_energy[0], row_energy[0], row_energy[1], row_energy[1]]))
    col_maps = regrouped([col_energy[0], col_energy[0], col_energy[1], col_energy[1]])
    col_std, col_inv = self_maps([jnp.where(other_image, swapped(m), m) for m in col_maps])

    levels = [weight_var / 27.0 * v + bias_var for v in box(cross)]
    for l in range(DEPTH):
        last = l == DEPTH - 1
        factor = weight_var / 1024.0 if last else weight_var / 9.0
        mapped = [
            relu_map(k, rs * cs, ri * ci, factor)
            for k, rs, cs, ri, ci in zip(levels, row_std[l], col_std[l], row_inv[l], col_inv[l])
        ]
        if not last:
            levels = [v + bias_var for v in box(mapped)]
    total = sum(mapped)
    total = total[:8] + total[8:]
    total = total + pltpu.roll(total, 4, 0)
    total = total + pltpu.roll(total, 2, 0)
    sub8 = sub[:8]
    a, s, b = sub8 % 2, sub8 // 2 % 2, sub8 // 4
    wanted = 2 * s + jnp.where(a == b, 0, 1)
    value = jnp.sum(jnp.where(group[:8] == wanted, total, 0.0), axis=1, keepdims=True) + bias_var
    value = jnp.broadcast_to(value, (8, LANES))
    result = jnp.where(lane[:8] == 0, value, pltpu.roll(value, 4, 0))
    for s in range(n_tiles):
        out_ref[s] = result[2 * s:2 * s + 2, 0:2]


def local(images, roots):
    n_row, n_col = lax.axis_size("row"), lax.axis_size("col")
    n_tiles = roots.shape[0]
    block, ch, pix = images.shape
    tiles = pix // LANES
    packed = images.reshape(block, ch, tiles, LANES).transpose(1, 2, 0, 3).reshape(ch * tiles * block, LANES)
    powers = n_row & (n_row - 1) == 0

    def row_target(i, k):
        return i ^ k if powers else (i + k) % n_row

    def row_source(row_index, root):
        return root ^ row_index if powers else lax.rem(row_index - root + n_row, n_row)

    def moved(value, target):
        pairs = []
        for i in range(n_row):
            for j in range(n_col):
                row, col = target(i, j)
                pairs.append((i * n_col + j, row * n_col + col))
        return lax.ppermute(value, ("row", "col"), pairs)

    def placed(value):
        return pltpu.with_memory_space_constraint(value, pltpu.VMEM)

    vmem = pl.BlockSpec(memory_space=pltpu.VMEM)
    single = pltpu.VMEM(packed.shape, jnp.float32)
    double = pltpu.VMEM((2 * packed.shape[0], LANES), jnp.float32)

    def on_core(body, out_shape, *values, flops=0):
        return pl.pallas_call(
            body, out_shape=out_shape, in_specs=[vmem] * len(values), out_specs=vmem, name=body.__name__,
            cost_estimate=pl.CostEstimate(flops=flops, bytes_accessed=0, transcendentals=0),
        )(*map(placed, values))

    near = moved(packed, lambda i, j: (i, j ^ 1))
    tile = on_core(blank, pltpu.VMEM((8, LANES), jnp.float32), flops=3000000)
    ahead, tile = lax.optimization_barrier((packed, tile))
    far = moved(ahead, lambda i, j: (i, ((j + 2) % n_col) ^ 1))
    both = on_core(join, double, packed, on_core(relay, single, near, flops=3000000), tile)
    pairs_in, slots = [], []
    for k in range(1, n_row - 1, 2):
        pairs_in.append(moved(both, lambda i, j, k=k: (row_target(i, k + 1 if j % 2 == 0 else k), j ^ 1)))
        slots += [(k, k + 1), (k + 1, k)]
    lone = []
    if n_row % 2 == 0:
        payload = on_core(relay, single, near, flops=20_000_000_000)
        lone.append(moved(payload, lambda i, j: (row_target(i, n_row - 1), j ^ 1)))
        slots.append((n_row - 1, n_row - 1))
    stack = pltpu.VMEM(((1 + len(pairs_in)) * packed.shape[0], LANES), jnp.float32)
    passed = moved(on_core(handed, stack, far, *pairs_in), lambda i, j: (i, j ^ 1))
    pick = pl.pallas_call(
        lambda *refs: prepare(row_source, slots, *refs),
        out_shape=pltpu.VMEM((n_tiles + 1, 8, LANES), jnp.int32),
        in_specs=[pl.BlockSpec(memory_space=pltpu.SMEM)],
        out_specs=vmem,
        cost_estimate=pl.CostEstimate(flops=20_000_000_000, bytes_accessed=0, transcendentals=0),
        name="prepare",
    )(roots)
    return pl.pallas_call(
        lambda *refs: kernel(n_tiles, *refs),
        out_shape=jax.ShapeDtypeStruct((n_tiles, block, block), jnp.float32),
        in_specs=[vmem] * (4 + len(pairs_in) + len(lone)),
        out_specs=vmem,
        name="tiles",
    )(*map(placed, [pick, far, passed, both, *pairs_in, *lone]))


def solution(mesh):
    in_specs = (P(("row", "col"), None, None), P())
    out_specs = P(None, "row", "col")
    return jax.shard_map(local, mesh=mesh, in_specs=in_specs, out_specs=out_specs, check_vma=False)
```

```python
import math

import jax
import jax.numpy as jnp
import numpy as np
from jax import lax
from jax.experimental import pallas as pl
from jax.experimental.pallas import tpu as pltpu
from jax.sharding import PartitionSpec as P

WIDTH = 32
LANES = 128
DEPTH = 4

weight_var = 2.0
bias_var = 0.1


def remainder_coefficients(degree=6, nodes=64):
    u = 0.5 + 0.5 * np.cos(np.pi * (np.arange(nodes) + 0.5) / nodes)
    angle = 2.0 * np.arcsin(np.sqrt(0.5 * u))
    series = sum(
        (-1) ** n * 2.0 * n / math.factorial(2 * n + 1) * angle ** (2 * n + 1) * -1.0
        for n in range(1, 8)
    )
    exact = np.sin(angle) - angle * np.cos(angle)
    q = np.where(angle < 0.5, series, exact) / u**1.5
    fit = np.polynomial.chebyshev.Chebyshev.fit(u, q, degree, domain=[0.0, 1.0])
    return fit.convert(kind=np.polynomial.Polynomial).coef


COEFS = [float(v) / (2.0 * math.pi) for v in remainder_coefficients()]


def join(own_ref, near_ref, tile_ref, both_out):
    rows = own_ref.shape[0]
    both_out[pl.ds(0, rows)] = own_ref[...]
    both_out[pl.ds(rows, rows)] = near_ref[...]


def blank(out):
    out[...] = jnp.zeros(out.shape, out.dtype)


def relay(near_ref, near_out):
    near_out[...] = near_ref[...]


def handed(far_ref, *refs):
    pair_refs, out = refs[:-1], refs[-1]
    rows = far_ref.shape[0]
    out[pl.ds(0, rows)] = far_ref[...]
    for n, ref in enumerate(pair_refs, 1):
        out[pl.ds(n * rows, rows)] = ref[pl.ds(0, rows)]


def prepare(row_source, slots, roots_ref, pick_out):
    n_tiles = roots_ref.shape[0]
    row_index, col_index = lax.axis_index("row"), lax.axis_index("col")
    odd = lax.rem(col_index, 2)
    for s in range(n_tiles):
        source = row_source(row_index, roots_ref[s, col_index])
        slot = jnp.int32(0)
        for n, (on_even, on_odd) in enumerate(slots, 1):
            slot = jnp.where(source == jnp.where(odd == 1, on_odd, on_even), n, slot)
        pick_out[s] = jnp.full((8, LANES), slot, jnp.int32)
    pick_out[n_tiles] = jnp.full((8, LANES), odd, jnp.int32)


def kernel(n_tiles, pick_ref, far_ref, passed_ref, both_ref, *refs):
    row_refs, out_ref = refs[:-1], refs[-1]
    block = far_ref.shape[0] // 24
    rows, bands = 8 * block, LANES // WIDTH
    sub = lax.broadcasted_iota(jnp.int32, (rows, LANES), 0)
    lane = lax.broadcasted_iota(jnp.int32, (rows, LANES), 1)
    not_left, not_right = (lane % WIDTH) != 0, (lane % WIDTH) != WIDTH - 1
    first_rows, last_rows = sub < block, sub >= rows - block
    even = (sub % 2) == 0
    group = lane // WIDTH
    other_image = (group % 2) == 1

    def box(maps):
        before = jnp.where(first_rows, 0.0, pltpu.roll(maps[-1], block, 0))
        after = jnp.where(last_rows, 0.0, pltpu.roll(maps[0], rows - block, 0))
        padded = [before] + maps + [after]
        sums = []
        for q in range(bands):
            down = padded[q] + padded[q + 1] + padded[q + 2]
            left = jnp.where(not_left, pltpu.roll(down, 1, 1), 0.0)
            right = jnp.where(not_right, pltpu.roll(down, LANES - 1, 1), 0.0)
            sums.append(down + left + right)
        return sums

    def swapped(m):
        return jnp.where(even, pltpu.roll(m, rows - 1, 0), pltpu.roll(m, 1, 0))

    def channels(value):
        return [value[c * rows:(c + 1) * rows] for c in range(3)]

    def regrouped(maps):
        turned = {}
        for b, m in enumerate(maps):
            for q in range(bands):
                shift = (b - q) % bands * WIDTH
                if (id(m), shift) not in turned:
                    turned[id(m), shift] = pltpu.roll(m, shift, 1) if shift else m
        out = []
        for q in range(bands):
            parts = [turned[id(m), (b - q) % bands * WIDTH] for b, m in enumerate(maps)]
            value = parts[-1]
            for b in range(bands - 2, -1, -1):
                value = jnp.where(group == b, parts[b], value)
            out.append(value)
        return out

    def self_maps(energy):
        levels = [[weight_var / 27.0 * v + bias_var for v in box(energy)]]
        for _ in range(DEPTH - 1):
            levels.append([weight_var / 18.0 * v + bias_var for v in box(levels[-1])])
        inverse = [[lax.rsqrt(v) for v in level] for level in levels]
        return [[v * r for v, r in zip(*pair)] for pair in zip(levels, inverse)], inverse

    def relu_map(k, scale, inverse, factor):
        u = jnp.maximum(1.0 - jnp.abs(k * inverse), 1e-30)
        u2 = u * u
        root = lax.rsqrt(u)
        a = [factor * v for v in COEFS]
        poly = (a[0] + a[1] * u) + (a[2] + a[3] * u) * u2 + ((a[4] + a[5] * u) + a[6] * u2) * (u2 * u2)
        return (0.5 * factor) * jnp.maximum(k, 0.0) + (scale * u2) * poly * root

    def chosen(flags, first, second):
        first, second = first.reshape(-1, 8, LANES), second.reshape(-1, 8, LANES)
        return jnp.where(flags[None], first, second).reshape(-1, LANES)

    odd = pick_ref[n_tiles] == 1
    cols = [channels(chosen(odd, both_ref[pl.ds(3 * rows, 3 * rows)], far_ref[...])), channels(passed_ref[pl.ds(0, 3 * rows)])]
    row_blocks = []
    for n in range(passed_ref.shape[0] // (3 * rows) - 1):
        row_blocks += [(row_refs[n], 3 * rows), (passed_ref, (n + 1) * 3 * rows)]
    row_blocks += [(ref, 0) for ref in row_refs[len(row_blocks) // 2:]]
    row_values = []
    for s in range(n_tiles):
        value = both_ref[pl.ds(0, 3 * rows)]
        for n, (ref, at) in enumerate(row_blocks, 1):
            value = chosen(pick_ref[s] == n, ref[pl.ds(at, 3 * rows)], value)
        row_values.append(channels(value))

    def dot(first, second):
        return sum(a * b for a, b in zip(first, second))

    turned_cols = [[swapped(v) for v in col] for col in cols]
    cross = regrouped([dot(r, c) for s, r in enumerate(row_values) for c in (cols[s], turned_cols[s])])
    row_energy = [dot(r, r) for r in row_values]
    col_energy = [dot(c, c) for c in cols]
    row_std, row_inv = self_maps(regrouped([row_energy[0], row_energy[0], row_energy[1], row_energy[1]]))
    col_maps = regrouped([col_energy[0], col_energy[0], col_energy[1], col_energy[1]])
    col_std, col_inv = self_maps([jnp.where(other_image, swapped(m), m) for m in col_maps])

    levels = [weight_var / 27.0 * v + bias_var for v in box(cross)]
    for l in range(DEPTH):
        last = l == DEPTH - 1
        factor = weight_var / 1024.0 if last else weight_var / 9.0
        mapped = [
            relu_map(k, rs * cs, ri * ci, factor)
            for k, rs, cs, ri, ci in zip(levels, row_std[l], col_std[l], row_inv[l], col_inv[l])
        ]
        if not last:
            levels = [v + bias_var for v in box(mapped)]
    total = sum(mapped)
    total = total[:8] + total[8:]
    total = total + pltpu.roll(total, 4, 0)
    total = total + pltpu.roll(total, 2, 0)
    sub8 = sub[:8]
    a, s, b = sub8 % 2, sub8 // 2 % 2, sub8 // 4
    wanted = 2 * s + jnp.where(a == b, 0, 1)
    value = jnp.sum(jnp.where(group[:8] == wanted, total, 0.0), axis=1, keepdims=True) + bias_var
    value = jnp.broadcast_to(value, (8, LANES))
    result = jnp.where(lane[:8] == 0, value, pltpu.roll(value, 4, 0))
    for s in range(n_tiles):
        out_ref[s] = result[2 * s:2 * s + 2, 0:2]


def local(images, roots):
    n_row, n_col = lax.axis_size("row"), lax.axis_size("col")
    n_tiles = roots.shape[0]
    block, ch, pix = images.shape
    tiles = pix // LANES
    packed = images.reshape(block, ch, tiles, LANES).transpose(1, 2, 0, 3).reshape(ch * tiles * block, LANES)
    powers = n_row & (n_row - 1) == 0

    def row_target(i, k):
        return i ^ k if powers else (i + k) % n_row

    def row_source(row_index, root):
        return root ^ row_index if powers else lax.rem(row_index - root + n_row, n_row)

    def moved(value, target):
        pairs = []
        for i in range(n_row):
            for j in range(n_col):
                row, col = target(i, j)
                pairs.append((i * n_col + j, row * n_col + col))
        return lax.ppermute(value, ("row", "col"), pairs)

    def placed(value):
        return pltpu.with_memory_space_constraint(value, pltpu.VMEM)

    vmem = pl.BlockSpec(memory_space=pltpu.VMEM)
    single = pltpu.VMEM(packed.shape, jnp.float32)
    double = pltpu.VMEM((2 * packed.shape[0], LANES), jnp.float32)

    def on_core(body, out_shape, *values, flops=0):
        return pl.pallas_call(
            body, out_shape=out_shape, in_specs=[vmem] * len(values), out_specs=vmem, name=body.__name__,
            cost_estimate=pl.CostEstimate(flops=flops, bytes_accessed=0, transcendentals=0),
        )(*map(placed, values))

    near = moved(packed, lambda i, j: (i, j ^ 1))
    tile = on_core(blank, pltpu.VMEM((8, LANES), jnp.float32), flops=3000000)
    ahead, tile = lax.optimization_barrier((packed, tile))
    far = moved(ahead, lambda i, j: (i, ((j + 2) % n_col) ^ 1))
    both = on_core(join, double, packed, on_core(relay, single, near, flops=3000000), tile)
    pairs_in, slots = [], []
    for k in range(2, n_row, 2):
        pairs_in.append(moved(both, lambda i, j, k=k: (row_target(i, k + 1 if j % 2 == 0 else k), j ^ 1)))
        slots += [(k, k + 1), (k + 1, k)]
    lone = []
    if n_row % 2 == 0:
        payload = on_core(relay, single, near, flops=20_000_000_000)
        lone.append(moved(payload, lambda i, j: (row_target(i, 1), j ^ 1)))
        slots.append((1, 1))
    stack = pltpu.VMEM(((1 + len(pairs_in)) * packed.shape[0], LANES), jnp.float32)
    passed = moved(on_core(handed, stack, far, *pairs_in), lambda i, j: (i, j ^ 1))
    pick = pl.pallas_call(
        lambda *refs: prepare(row_source, slots, *refs),
        out_shape=pltpu.VMEM((n_tiles + 1, 8, LANES), jnp.int32),
        in_specs=[pl.BlockSpec(memory_space=pltpu.SMEM)],
        out_specs=vmem,
        cost_estimate=pl.CostEstimate(flops=20_000_000_000, bytes_accessed=0, transcendentals=0),
        name="prepare",
    )(roots)
    return pl.pallas_call(
        lambda *refs: kernel(n_tiles, *refs),
        out_shape=jax.ShapeDtypeStruct((n_tiles, block, block), jnp.float32),
        in_specs=[vmem] * (4 + len(pairs_in) + len(lone)),
        out_specs=vmem,
        name="tiles",
    )(*map(placed, [pick, far, passed, both, *pairs_in, *lone]))


def solution(mesh):
    in_specs = (P(("row", "col"), None, None), P())
    out_specs = P(None, "row", "col")
    return jax.shard_map(local, mesh=mesh, in_specs=in_specs, out_specs=out_specs, check_vma=False)
```
